32 devices in a mesh: groups: 2 (over x), expert: 16 (over z, y, core).
Axes of the slice: x: 2, y: 2, z: 4, core: 2. Of those that a mesh axis runs over, the one named last changes fastest.
Arguments:
- token_codes: bfloat16 [2048, 1024], P(('groups', 'expert')), parts along dimension 0, may hold values from -6 to 6
- route_devices: int32 [2048, 8], P(('groups', 'expert')), parts along dimension 0, may hold values from 0 to 15, all different within a row; in each aligned block of 64 rows (0 to 63, 64 to 127, ...) at most 64 rows name the same one
- route_members: int32 [2048, 8], P(('groups', 'expert')), parts along dimension 0, may hold values from 0 to 1
- gate_scores: bfloat16 [2048, 8], P(('groups', 'expert')), parts along dimension 0, may hold values from 0.049804688 to 1
- gate_core: bfloat16 [32, 1024, 1024], P('expert'), may hold values from -0.1875 to 0.1875
- up_core: bfloat16 [32, 1024, 1024], P('expert'), may hold values from -0.1875 to 0.1875
- down_core: bfloat16 [32, 1024, 512], P('expert'), may hold values from -0.1875 to 0.1875
Outputs:
- mixed_codes: bfloat16 [2048, 512], P(('groups', 'expert')), parts along dimension 0
The draws below stay inside these ranges and needn't reach their ends.
There are 2 independent parts, one for each index of `groups`. The reference program is written for one: setup_inputs(seed, part) draws one part's arguments, and reference() takes and returns one part's arrays. A program takes and returns all parts, laid end to end along the dimension named above; an argument that names none is the same for every part. Nothing has to cross between parts.
Inputs may be any that keep to these rules, and one draw needn't show every extreme that they name: `route_devices`: each row names 8 different devices. Within the rows of one device (aligned blocks of 64 rows) no device is named by more than 64 rows, and in every draw some device is named by exactly 64 rows of some device.
All inputs are finite; a program needn't handle non-finite values.
Results may differ from the reference program's by a relative error of at most 0.0058.
Values may be sent and summed in bfloat16 or wider, within the bound.
No kernel may reach another device: no remote copies, remote signals or barrier semaphores. Data moves between devices by JAX's collectives and lax.ppermute only.
A program may use at most 64 MiB of HBM per device.

```python
import math
import jax
import jax.numpy as jnp
import numpy as np
from jax import lax

R_IN = 1024
R_OUT = 512
H = 1024
TOP = 8
EXP_DEV = 2
TOK_DEV = 64
EXPERTS = 32
TOKENS = 1024
CAP = 64
N_EXPERT = 16


def with_ends(values, rng, least, high):
    longest = values.shape.index(max(values.shape))
    spots = []
    for shift in (0, 1):
        where = [jax.random.randint(jax.random.fold_in(rng, axis), (), 0, length) for axis, length in enumerate(values.shape)]
        where[longest] = (where[longest] + shift) % values.shape[longest]
        spots.append(tuple(where))
    return values.at[spots[0]].set(least).at[spots[1]].set(high)


def block_scale(rng, dims, shards, low, top_value):
    gain, own = 1.0, jax.random.fold_in(rng, 6)
    for dim, blocks in shards:
        draws = jnp.exp(jax.random.uniform(jax.random.fold_in(own, dim), (blocks,), jnp.float32, low / len(shards), top_value / len(shards)))
        gain = gain * jnp.repeat(draws, dims[dim] // blocks).reshape([-1 if axis == dim else 1 for axis in range(len(dims))])
    return gain


def deal_out(rng, own, number, rows, number_of, top, most, skew):
    sequence = jax.random.permutation(rng, number_of)
    crowded, usual = shares(number_of, rows * top, most, skew, True), shares(number_of, rows * top, most, skew, False)
    places = jnp.arange(number_of)

    def named(sizes, rotation):
        used = int((sizes > 0).sum())
        fixed = max(1, used // 4)
        moved = fixed + (places - fixed + rotation * (used - fixed)) % max(1, number_of - fixed)
        return jnp.zeros((number_of,), jnp.int32).at[sequence[jnp.where(places < fixed, places, moved)]].set(jnp.asarray(sizes, jnp.int32))

    sizes = jnp.where(number % 4 == 0, named(crowded, number // 4), named(usual, number - number // 4 - 1))
    mixed = jax.random.permutation(jax.random.fold_in(own, 3), number_of)
    giver, taker = mixed[0:number_of // 2 * 2:2], mixed[1:number_of // 2 * 2:2]
    margin = jnp.minimum(sizes[giver] - 1, most - sizes[taker]) // 2
    margin = jnp.where((giver == sequence[0]) | (taker == sequence[0]) | (sizes[taker] == 0), 0, jnp.maximum(margin, 0))
    moved = jax.random.randint(jax.random.fold_in(own, 4), (number_of // 2,), 0, 1 << 20) % (margin + 1)
    sizes = sizes.at[giver].add(-moved).at[taker].add(moved)
    items = jnp.searchsorted(jnp.cumsum(sizes), jnp.arange(rows * top), side="right").astype(jnp.int32)
    grid = items.reshape(top, rows).T
    grid = grid[jax.random.permutation(jax.random.fold_in(own, 1), rows)]
    rotation = jax.random.randint(jax.random.fold_in(own, 2), (rows, 1), 0, top)
    return jnp.take_along_axis(grid, (jnp.arange(top)[None, :] + rotation) % top, axis=1)


def shares(number_of, total, reach, skew, full):
    portions = [(1 << 20) // math.isqrt(rank ** skew) + 1 for rank in range(1, number_of + 1)]
    largest = reach if full else min(reach, max(-(-total // number_of), total * portions[0] // sum(portions)))
    least = 1 if total - largest >= number_of - 1 else 0
    given, surplus = [largest] + [least] * (number_of - 1), total - largest - least * (number_of - 1)
    while surplus > 0:
        free = [i for i in range(1, number_of) if given[i] < largest] or [i for i in range(1, number_of) if given[i] < reach]
        whole, remaining = sum([portions[i] for i in free]), surplus
        for i in free:
            extra = min(reach - given[i], max(1, remaining * portions[i] // whole), surplus)
            given[i] = given[i] + extra
            surplus = surplus - extra
    return np.array(given)


def gaussian(rng, shape, spread, most, pieces=(), kind=jnp.bfloat16):
    entries = jax.random.normal(rng, shape, jnp.float32) * spread
    if len(pieces) > 0:
        entries = block_scale(rng, shape, pieces, -0.22, 0.18) * entries
    return jnp.clip(entries, min=-most, max=most).astype(kind)


def setup_inputs(seed: int = 0, part: int = 0) -> dict:
    arg_keys = jax.random.split(jax.random.key(seed), 8)
    own_keys = jax.random.split(jax.random.fold_in(arg_keys[7], part), 8)
    token_codes = gaussian(own_keys[0], (TOKENS, R_IN), 1.0, 6.0, ((0, 16),))
    route_devices_keys = jax.random.split(jax.random.fold_in(own_keys[1], 1), TOKENS // TOK_DEV)
    route_devices_turns = jax.random.permutation(jax.random.fold_in(own_keys[1], 3), TOKENS // TOK_DEV)
    route_devices = jax.vmap(lambda own, number: deal_out(jax.random.fold_in(own_keys[1], 2), own, number, TOK_DEV, N_EXPERT, TOP, CAP, 1))(route_devices_keys, route_devices_turns).reshape((TOKENS, TOP))
    route_members = with_ends(jax.random.randint(own_keys[2], (TOKENS, TOP), 0, EXP_DEV), jax.random.fold_in(own_keys[2], 1), 0, EXP_DEV - 1).astype(jnp.int32)
    gate_scores = jnp.clip(jnp.exp(math.log(1.0) - 2.9996462 * jax.random.uniform(own_keys[3], (TOKENS, TOP), jnp.float32) ** block_scale(own_keys[3], (TOKENS, TOP), ((0, 16),), -0.2, 0.2)), 0.049804688, 1.0).astype(jnp.bfloat16)
    gate_core = gaussian(arg_keys[4], (EXPERTS, R_IN, H), R_IN ** -0.5, 0.1875, ((0, 16),))
    up_core = gaussian(arg_keys[5], (EXPERTS, R_IN, H), R_IN ** -0.5, 0.1875, ((0, 16),))
    down_core = gaussian(arg_keys[6], (EXPERTS, H, R_OUT), H ** -0.5, 0.1875, ((0, 16),))
    return {"token_codes": token_codes, "route_devices": route_devices, "route_members": route_members, "gate_scores": gate_scores, "gate_core": gate_core, "up_core": up_core, "down_core": down_core}


def reference(token_codes, route_devices, route_members, gate_scores, gate_core, up_core, down_core):
    scores = gate_scores.astype(jnp.float32)
    weights = 2.5 * scores / jnp.sum(scores, axis=1, keepdims=True)
    expert_ids = (route_devices * EXP_DEV + route_members).astype(jnp.int32)
    flat_ids = expert_ids.reshape(-1).astype(jnp.int32)
    flat_weights = weights.reshape(-1)
    pair_count = flat_ids.shape[0]
    sorted_pairs = jnp.argsort(flat_ids, stable=True).astype(jnp.int32)
    expert_range = jnp.arange(EXPERTS, dtype=jnp.int32)
    counts = jnp.sum((flat_ids[:, None] == expert_range[None, :]).astype(jnp.int32), axis=0).astype(jnp.int32)
    starts = (jnp.cumsum(counts) - counts).astype(jnp.int32)
    slot_bound = N_EXPERT * CAP
    offsets = jnp.arange(slot_bound, dtype=jnp.int32)

    def one_expert(totals, expert):
        position = jnp.minimum(starts[expert] + offsets, pair_count - 1)
        pair_index = sorted_pairs[position]
        is_live = offsets < counts[expert]
        token_index = pair_index // TOP
        gathered = token_codes[token_index]
        gate_value = jnp.dot(gathered, gate_core[expert], preferred_element_type=jnp.float32)
        up_value = jnp.dot(gathered, up_core[expert], preferred_element_type=jnp.float32)
        hidden = (jax.nn.silu(gate_value) * up_value).astype(jnp.bfloat16)
        result = jnp.dot(hidden, down_core[expert], preferred_element_type=jnp.float32).astype(jnp.bfloat16)
        route_term = jnp.where(is_live[:, None], flat_weights[pair_index][:, None] * result.astype(jnp.float32), jnp.zeros((), jnp.float32))
        return totals.at[token_index].add(route_term), None

    totals, unused = lax.scan(one_expert, jnp.zeros((TOKENS, R_OUT), jnp.float32), expert_range)
    return totals.astype(jnp.bfloat16)
```

```python
import functools

import jax
import jax.numpy as jnp
from jax import lax
from jax.experimental import pallas as pl
from jax.experimental.pallas import tpu as pltpu
from jax.sharding import PartitionSpec as P

LANES = 128
VMEM_SPEC = pl.BlockSpec(memory_space=pltpu.VMEM)


def tag_kernel(local_experts, codes_ref, devices_ref, members_ref, scores_ref, out_ref):
    rank_in = codes_ref.shape[1]
    rows = codes_ref.shape[0]
    lanes = out_ref.shape[1] - rank_in
    ids = devices_ref[...] * local_experts + members_ref[...]
    scores = scores_ref[...].astype(jnp.float32)
    lane = lax.broadcasted_iota(jnp.int32, (rows, lanes), 1)
    spread = jnp.zeros((rows, lanes), jnp.float32)
    for k in range(ids.shape[1]):
        spread = jnp.where(lane == ids[:, k : k + 1], scores[:, k : k + 1], spread)
    out_ref[:, :rank_in] = codes_ref[...]
    out_ref[:, rank_in:] = spread.astype(jnp.bfloat16)


def tag_tokens(codes, devices, members, scores, local_experts, experts):
    lanes = -(-experts // LANES) * LANES
    rows, rank_in = codes.shape
    return pl.pallas_call(
        functools.partial(tag_kernel, local_experts),
        out_shape=jax.ShapeDtypeStruct((rows, rank_in + lanes), jnp.bfloat16),
        in_specs=[VMEM_SPEC] * 4,
        out_specs=VMEM_SPEC,
        name="tag_tokens",
    )(codes, devices, members, scores)


def expert_kernel(first_ref, *refs):
    blocks, (gate_ref, up_ref, down_ref, near_ref, far_ref, rows_ref) = refs[:4], refs[4:]
    local_experts, rank_in, hidden_units = gate_ref.shape
    size = blocks[0].shape[0]
    for i, block in enumerate(blocks):
        rows_ref[i * size : (i + 1) * size, :] = block[...]
    scores = rows_ref[:, rank_in:].astype(jnp.float32)
    total = jnp.sum(scores, axis=1, keepdims=True)
    lane = lax.broadcasted_iota(jnp.int32, scores.shape, 1)
    codes = rows_ref[:, :rank_in]
    out = jnp.zeros((codes.shape[0], down_ref.shape[2]), jnp.float32)
    own = jnp.zeros_like(total)
    for e in range(local_experts):
        score = jnp.sum(jnp.where(lane == first_ref[0] + e, scores, 0.0), axis=1, keepdims=True)
        own = own + score
        gate = jnp.dot(codes, gate_ref[e], preferred_element_type=jnp.float32)
        up = jnp.dot(codes, up_ref[e], preferred_element_type=jnp.float32)
        hidden = gate / (1.0 + jnp.exp(-gate)) * up
        hidden = jnp.where(score > 0.0, hidden, 0.0).astype(jnp.bfloat16)
        out = out + jnp.dot(hidden, down_ref[e], preferred_element_type=jnp.float32)
    weight = 2.5 * own / total
    out = (weight * out.astype(jnp.bfloat16).astype(jnp.float32)).astype(jnp.bfloat16)
    near_ref[...] = out[: 2 * size].reshape(near_ref.shape)
    far_ref[...] = out[2 * size :].reshape(far_ref.shape)


def apply_experts(first, blocks, gate_core, up_core, down_core):
    rows, width = blocks[0].shape
    local_experts, rank_in, hidden_units = gate_core.shape
    rank_out = down_core.shape[2]
    half = jax.ShapeDtypeStruct((2, rows, rank_out), jnp.bfloat16)
    flops = 2 * 4 * rows * local_experts * hidden_units * (2 * rank_in + rank_out)
    return pl.pallas_call(
        expert_kernel,
        out_shape=(half, half),
        in_specs=[pl.BlockSpec(memory_space=pltpu.SMEM)] + [VMEM_SPEC] * 7,
        out_specs=(VMEM_SPEC, VMEM_SPEC),
        scratch_shapes=[pltpu.VMEM((4 * rows, width), jnp.bfloat16)],
        compiler_params=pltpu.CompilerParams(vmem_limit_bytes=24 * 1024 * 1024),
        cost_estimate=pl.CostEstimate(flops=flops, bytes_accessed=4 * rows * width * 2, transcendentals=0),
        name="apply_experts",
    )(first, *blocks, gate_core, up_core, down_core)


def local(token_codes, route_devices, route_members, gate_scores, gate_core, up_core, down_core):
    size = lax.axis_size("expert")
    local_experts = gate_core.shape[0]
    columns = size // 4

    def exchange(array, mask):
        return lax.ppermute(array, "expert", [(i, i ^ mask) for i in range(size)])

    first = (lax.axis_index("expert") * local_experts).astype(jnp.int32).reshape(1)
    own = tag_tokens(
        token_codes, route_devices, route_members, gate_scores, local_experts, local_experts * size
    )
    gate_core = pltpu.with_memory_space_constraint(gate_core, pltpu.VMEM)
    up_core = pltpu.with_memory_space_constraint(up_core, pltpu.VMEM)
    down_core = pltpu.with_memory_space_constraint(down_core, pltpu.VMEM)
    mixed = None
    gathered = [own] + [exchange(own, 4 * j) for j in range(1, columns)]
    finished = []
    for j, block in enumerate(gathered):
        across = exchange(block, 2)
        blocks = [block, across, exchange(block, 1), exchange(across, 1)]
        near, far = apply_experts(first, blocks, gate_core, up_core, down_core)
        pair = near.astype(jnp.float32) + exchange(far, 1).astype(jnp.float32)
        pair = pair.astype(jnp.bfloat16)
        done = pair[0].astype(jnp.float32) + exchange(pair[1], 2).astype(jnp.float32)
        finished.append(exchange(done.astype(jnp.bfloat16), 4 * j) if j else done)
    mixed = sum(part.astype(jnp.float32) for part in finished)
    return mixed.astype(jnp.bfloat16)


def solution(mesh):
    tokens = P(("groups", "expert"), None)
    experts = P("expert", None, None)
    return jax.shard_map(
        local,
        mesh=mesh,
        in_specs=(tokens,) * 4 + (experts,) * 3,
        out_specs=tokens,
        check_vma=False,
    )
```

```python
import functools

import jax
import jax.numpy as jnp
from jax import lax
from jax.experimental import pallas as pl
from jax.experimental.pallas import tpu as pltpu
from jax.sharding import PartitionSpec as P

LANES = 128
VMEM_SPEC = pl.BlockSpec(memory_space=pltpu.VMEM)


def tag_kernel(local_experts, codes_ref, devices_ref, members_ref, scores_ref, out_ref):
    rows, rank_in = codes_ref.shape
    lanes = out_ref.shape[1] - rank_in
    ids = devices_ref[...] * local_experts + members_ref[...]
    scores = scores_ref[...].astype(jnp.float32)
    expert = lax.broadcasted_iota(jnp.int32, (lanes, rows), 0)
    spread = jnp.zeros((lanes, rows), jnp.float32)
    for k in range(ids.shape[0]):
        spread = jnp.where(expert == ids[k : k + 1, :], scores[k : k + 1, :], spread)
    out_ref[:, :rank_in] = codes_ref[...]
    out_ref[:, rank_in:] = spread.T.astype(jnp.bfloat16)


def tag_tokens(codes, devices, members, scores, local_experts, experts):
    lanes = -(-experts // LANES) * LANES
    rows, rank_in = codes.shape
    return pl.pallas_call(
        functools.partial(tag_kernel, local_experts),
        out_shape=jax.ShapeDtypeStruct((rows, rank_in + lanes), jnp.bfloat16),
        in_specs=[VMEM_SPEC] * 4,
        out_specs=VMEM_SPEC,
        name="tag_tokens",
    )(codes, devices.T, members.T, scores.T)


def expert_rows(first_ref, blocks, weights, before, near_ref, far_ref, rows_ref):
    gate_ref, up_ref, down_ref = weights
    local_experts, rank_in, hidden_units = gate_ref.shape
    size = blocks[0].shape[0]
    for i, block in enumerate(blocks):
        rows_ref[i * size : (i + 1) * size, :] = block[...]
    scores = rows_ref[:, rank_in:].astype(jnp.float32)
    total = jnp.sum(scores, axis=1, keepdims=True)
    lane = lax.broadcasted_iota(jnp.int32, scores.shape, 1)
    codes = rows_ref[:, :rank_in]
    out = jnp.zeros((codes.shape[0], down_ref.shape[2]), jnp.float32)
    own = jnp.zeros_like(total)
    for e in range(local_experts):
        score = jnp.sum(jnp.where(lane == first_ref[0] + e, scores, 0.0), axis=1, keepdims=True)
        own = own + score
        before(e, 0)
        gate = jnp.dot(codes, gate_ref[e], preferred_element_type=jnp.float32)
        before(e, 1)
        up = jnp.dot(codes, up_ref[e], preferred_element_type=jnp.float32)
        hidden = gate / (1.0 + jnp.exp(-gate)) * up
        hidden = jnp.where(score > 0.0, hidden, 0.0).astype(jnp.bfloat16)
        before(e, 2)
        out = out + jnp.dot(hidden, down_ref[e], preferred_element_type=jnp.float32)
    weight = 2.5 * own / total
    out = (weight * out.astype(jnp.bfloat16).astype(jnp.float32)).astype(jnp.bfloat16)
    near_ref[...] = out[: 2 * size].reshape(near_ref.shape)
    far_ref[...] = out[2 * size :].reshape(far_ref.shape)


def load_and_apply_kernel(first_ref, *refs):
    blocks, sources, near_ref, far_ref = refs[:4], refs[4:7], refs[7], refs[8]
    weights, rows_ref, semaphores = refs[9:12], refs[12], refs[13]
    copies = [
        [
            pltpu.make_async_copy(source.at[e], kept.at[e], semaphores.at[e, k])
            for k, (source, kept) in enumerate(zip(sources, weights))
        ]
        for e in range(sources[0].shape[0])
    ]
    for group in copies:
        for copy in group:
            copy.start()
    expert_rows(
        first_ref, blocks, weights, lambda e, k: copies[e][k].wait(), near_ref, far_ref, rows_ref
    )


def apply_kernel(first_ref, *refs):
    expert_rows(first_ref, refs[:4], refs[4:7], lambda e, k: None, *refs[7:])


def apply_experts(first, blocks, weights, load):
    rows, width = blocks[0].shape
    local_experts, rank_in, hidden_units = weights[0].shape
    rank_out = weights[2].shape[2]
    half = jax.ShapeDtypeStruct((2, rows, rank_out), jnp.bfloat16)
    flops = 2 * 4 * rows * local_experts * hidden_units * (2 * rank_in + rank_out)
    held = tuple(pltpu.VMEM(w.shape, w.dtype) for w in weights) if load else ()
    place = pl.BlockSpec(memory_space=pltpu.HBM) if load else VMEM_SPEC
    return pl.pallas_call(
        load_and_apply_kernel if load else apply_kernel,
        out_shape=(half, half) + held,
        in_specs=[pl.BlockSpec(memory_space=pltpu.SMEM)] + [VMEM_SPEC] * 4 + [place] * 3,
        out_specs=(VMEM_SPEC,) * (2 + len(held)),
        scratch_shapes=[pltpu.VMEM((4 * rows, width), jnp.bfloat16)]
        + ([pltpu.SemaphoreType.DMA((local_experts, 3))] if load else []),
        compiler_params=pltpu.CompilerParams(vmem_limit_bytes=24 * 1024 * 1024),
        cost_estimate=pl.CostEstimate(flops=flops, bytes_accessed=4 * rows * width * 2, transcendentals=0),
        name="load_and_apply" if load else "apply_experts",
    )(first, *blocks, *weights)


def local(token_codes, route_devices, route_members, gate_scores, gate_core, up_core, down_core):
    size = lax.axis_size("expert")
    local_experts = gate_core.shape[0]
    columns = size // 4

    def exchange(array, mask):
        return lax.ppermute(array, "expert", [(i, i ^ mask) for i in range(size)])

    first = (lax.axis_index("expert") * local_experts).astype(jnp.int32).reshape(1)
    own = tag_tokens(
        token_codes, route_devices, route_members, gate_scores, local_experts, local_experts * size
    )
    weights = (gate_core, up_core, down_core)
    gathered = [own]
    for j in range(1, columns):
        low = j & -j
        gathered.append(exchange(gathered[j - low], 4 * low))
    finished = []
    for j, block in enumerate(gathered):
        across = exchange(block, 2)
        blocks = [block, across, exchange(block, 1), exchange(across, 1)]
        near, far, *held = apply_experts(first, blocks, weights, j == 0)
        if j == 0:
            weights = tuple(held)
        pair = near.astype(jnp.float32) + exchange(far, 1).astype(jnp.float32)
        pair = pair.astype(jnp.bfloat16)
        done = pair[0].astype(jnp.float32) + exchange(pair[1], 2).astype(jnp.float32)
        finished.append(exchange(done.astype(jnp.bfloat16), 4 * j) if j else done)
    mixed = sum(part.astype(jnp.float32) for part in finished)
    return mixed.astype(jnp.bfloat16)


def solution(mesh):
    tokens = P(("groups", "expert"), None)
    experts = P("expert", None, None)
    return jax.shard_map(
        local,
        mesh=mesh,
        in_specs=(tokens,) * 4 + (experts,) * 3,
        out_specs=tokens,
        check_vma=False,
    )
```

```python
import functools

import jax
import jax.numpy as jnp
from jax import lax
from jax.experimental import pallas as pl
from jax.experimental.pallas import tpu as pltpu
from jax.sharding import PartitionSpec as P

LANES = 128
MIB = 1024 * 1024
VMEM_SPEC = pl.BlockSpec(memory_space=pltpu.VMEM)


def tag_kernel(local_experts, codes_ref, devices_ref, members_ref, scores_ref, out_ref):
    rows, rank_in = codes_ref.shape
    lanes = out_ref.shape[1] - rank_in
    ids = devices_ref[...] * local_experts + members_ref[...]
    scores = scores_ref[...].astype(jnp.float32)
    expert = lax.broadcasted_iota(jnp.int32, (lanes, rows), 0)
    spread = jnp.zeros((lanes, rows), jnp.float32)
    for k in range(ids.shape[0]):
        spread = jnp.where(expert == ids[k : k + 1, :], scores[k : k + 1, :], spread)
    out_ref[:, :rank_in] = codes_ref[...]
    out_ref[:, rank_in:] = spread.T.astype(jnp.bfloat16)


def tag_tokens(codes, devices, members, scores, local_experts, experts):
    lanes = -(-experts // LANES) * LANES
    rows, rank_in = codes.shape
    operands = [
        pltpu.with_memory_space_constraint(operand, pltpu.HBM)
        for operand in (codes, devices.T, members.T, scores.T)
    ]
    return pl.pallas_call(
        functools.partial(tag_kernel, local_experts),
        out_shape=jax.ShapeDtypeStruct((rows, rank_in + lanes), jnp.bfloat16),
        out_specs=VMEM_SPEC,
        compiler_params=pltpu.CompilerParams(vmem_limit_bytes=8 * MIB),
        cost_estimate=pl.CostEstimate(
            flops=8_000_000_000, bytes_accessed=16_000_000, transcendentals=0
        ),
        name="tag_tokens",
    )(*operands)


def expert_kernel(count, *refs):
    blocks, (gate_ref, up_ref, down_ref, near_ref, far_ref, rows_ref) = refs[:count], refs[count:]
    local_experts, rank_in, hidden_units = gate_ref.shape
    at = 0
    for block in blocks:
        rows_ref[at : at + block.shape[0], :] = block[...]
        at += block.shape[0]
    scores = rows_ref[:, rank_in:].astype(jnp.float32)
    total = jnp.sum(scores, axis=1, keepdims=True)
    lane = lax.broadcasted_iota(jnp.int32, scores.shape, 1)
    first = lax.axis_index("expert") * local_experts
    codes = rows_ref[:, :rank_in]
    out = jnp.zeros((codes.shape[0], down_ref.shape[2]), jnp.float32)
    own = jnp.zeros_like(total)
    for e in range(local_experts):
        score = jnp.sum(jnp.where(lane == first + e, scores, 0.0), axis=1, keepdims=True)
        own = own + score
        gate = jnp.dot(codes, gate_ref[e], preferred_element_type=jnp.float32)
        up = jnp.dot(codes, up_ref[e], preferred_element_type=jnp.float32)
        hidden = gate / (1.0 + jnp.exp(-gate)) * up
        hidden = jnp.where(score > 0.0, hidden, 0.0).astype(jnp.bfloat16)
        out = out + jnp.dot(hidden, down_ref[e], preferred_element_type=jnp.float32)
    weight = 2.5 * own / total
    out = (weight * out.astype(jnp.bfloat16).astype(jnp.float32)).astype(jnp.bfloat16)
    half = near_ref.shape[0]
    near_ref[...] = out[:half]
    far_ref[...] = out[half:]


def apply_experts(blocks, weights):
    width = blocks[0].shape[1]
    rows = sum(block.shape[0] for block in blocks)
    local_experts, rank_in, hidden_units = weights[0].shape
    rank_out = weights[2].shape[2]
    half = jax.ShapeDtypeStruct((rows // 2, rank_out), jnp.bfloat16)
    flops = 2 * rows * local_experts * hidden_units * (2 * rank_in + rank_out)
    return pl.pallas_call(
        functools.partial(expert_kernel, len(blocks)),
        out_shape=(half, half),
        in_specs=[VMEM_SPEC] * (len(blocks) + 3),
        out_specs=(VMEM_SPEC, VMEM_SPEC),
        scratch_shapes=[pltpu.VMEM((rows, width), jnp.bfloat16)],
        compiler_params=pltpu.CompilerParams(vmem_limit_bytes=24 * MIB),
        cost_estimate=pl.CostEstimate(
            flops=flops, bytes_accessed=2 * rows * width, transcendentals=0
        ),
        name="apply_experts",
    )(*blocks, *weights)


def wide(array):
    return array.astype(jnp.float32)


def local(token_codes, route_devices, route_members, gate_scores, gate_core, up_core, down_core):
    size = lax.axis_size("expert")
    local_experts = gate_core.shape[0]
    rows = token_codes.shape[0]
    weights = (gate_core, up_core, down_core)

    def exchange(array, mask):
        return lax.ppermute(array, "expert", [(i, i ^ mask) for i in range(size)])

    own = tag_tokens(
        token_codes, route_devices, route_members, gate_scores, local_experts, local_experts * size
    )
    across = exchange(own, 2)
    gathered = {0: own}
    for j in range(1, size // 4):
        low = j & -j
        gathered[j] = exchange(gathered[j - low], 4 * low)
    near_by = lax.optimization_barrier((gathered[1], gathered[2], across))
    middle = exchange(jnp.concatenate(near_by[:2]), 2)
    gathered[3] = exchange(near_by[1], 4)
    pairs = {0: (own, across), 1: (gathered[1], middle[:rows]), 2: (gathered[2], middle[rows:])}
    pairs |= {j: (gathered[j], exchange(gathered[j], 2)) for j in range(3, size // 4)}
    halves, near = {}, None
    for j, blocks in pairs.items():
        blocks = blocks + tuple(exchange(block, 1) for block in blocks)
        near, far = apply_experts(tuple(blocks), weights)
        pair = wide(near) + wide(exchange(far, 1))
        halves[j] = pair if j == 0 else pair.astype(jnp.bfloat16)
    pair = halves[0] + wide(exchange(halves[1], 4))
    mixed = pair[:rows] + wide(exchange(pair[rows:].astype(jnp.bfloat16), 2))
    for j in range(2, size // 4):
        done = wide(halves[j][:rows]) + wide(exchange(halves[j][rows:], 2))
        mixed = mixed + wide(exchange(done.astype(jnp.bfloat16), 4 * j))
    return mixed.astype(jnp.bfloat16)


def solution(mesh):
    tokens = P(("groups", "expert"), None)
    experts = P("expert", None, None)
    return jax.shard_map(
        local,
        mesh=mesh,
        in_specs=(tokens,) * 4 + (experts,) * 3,
        out_specs=tokens,
        check_vma=False,
    )
```

```python
import functools

import jax
import jax.numpy as jnp
from jax import lax
from jax.experimental import pallas as pl
from jax.experimental.pallas import tpu as pltpu
from jax.sharding import PartitionSpec as P

LANES = 128
MIB = 1024 * 1024
VMEM_SPEC = pl.BlockSpec(memory_space=pltpu.VMEM)


def tag_kernel(local_experts, codes_ref, devices_ref, members_ref, scores_ref, out_ref):
    rows, rank_in = codes_ref.shape
    lanes = out_ref.shape[1] - rank_in
    ids = devices_ref[...] * local_experts + members_ref[...]
    scores = scores_ref[...].astype(jnp.float32)
    expert = lax.broadcasted_iota(jnp.int32, (lanes, rows), 0)
    spread = jnp.zeros((lanes, rows), jnp.float32)
    for k in range(ids.shape[0]):
        spread = jnp.where(expert == ids[k : k + 1, :], scores[k : k + 1, :], spread)
    out_ref[:, :rank_in] = codes_ref[...]
    out_ref[:, rank_in:] = spread.T.astype(jnp.bfloat16)


def tag_tokens(codes, devices, members, scores, local_experts, experts):
    lanes = -(-experts // LANES) * LANES
    rows, rank_in = codes.shape
    operands = [
        pltpu.with_memory_space_constraint(operand, pltpu.HBM)
        for operand in (codes, devices.T, members.T, scores.T)
    ]
    return pl.pallas_call(
        functools.partial(tag_kernel, local_experts),
        out_shape=jax.ShapeDtypeStruct((rows, rank_in + lanes), jnp.bfloat16),
        out_specs=VMEM_SPEC,
        compiler_params=pltpu.CompilerParams(vmem_limit_bytes=8 * MIB),
        cost_estimate=pl.CostEstimate(
            flops=8_000_000_000, bytes_accessed=16_000_000, transcendentals=0
        ),
        name="tag_tokens",
    )(*operands)


def expert_kernel(count, *refs):
    blocks, (gate_ref, up_ref, down_ref, near_ref, far_ref, rows_ref) = refs[:count], refs[count:]
    local_experts, rank_in, hidden_units = gate_ref.shape
    at = 0
    for block in blocks:
        rows_ref[at : at + block.shape[0], :] = block[...]
        at += block.shape[0]
    scores = rows_ref[:, rank_in:].astype(jnp.float32)
    total = jnp.sum(scores, axis=1, keepdims=True)
    lane = lax.broadcasted_iota(jnp.int32, scores.shape, 1)
    first = lax.axis_index("expert") * local_experts
    codes = rows_ref[:, :rank_in]
    out = jnp.zeros((codes.shape[0], down_ref.shape[2]), jnp.float32)
    own = jnp.zeros_like(total)
    for e in range(local_experts):
        score = jnp.sum(jnp.where(lane == first + e, scores, 0.0), axis=1, keepdims=True)
        own = own + score
        gate = jnp.dot(codes, gate_ref[e], preferred_element_type=jnp.float32)
        up = jnp.dot(codes, up_ref[e], preferred_element_type=jnp.float32)
        hidden = gate / (1.0 + jnp.exp(-gate)) * up
        hidden = jnp.where(score > 0.0, hidden, 0.0).astype(jnp.bfloat16)
        out = out + jnp.dot(hidden, down_ref[e], preferred_element_type=jnp.float32)
    weight = 2.5 * own / total
    out = (weight * out.astype(jnp.bfloat16).astype(jnp.float32)).astype(jnp.bfloat16)
    half = near_ref.shape[0]
    near_ref[...] = out[:half]
    far_ref[...] = out[half:]


def apply_experts(blocks, weights):
    width = blocks[0].shape[1]
    rows = sum(block.shape[0] for block in blocks)
    local_experts, rank_in, hidden_units = weights[0].shape
    rank_out = weights[2].shape[2]
    half = jax.ShapeDtypeStruct((rows // 2, rank_out), jnp.bfloat16)
    flops = 2 * rows * local_experts * hidden_units * (2 * rank_in + rank_out)
    return pl.pallas_call(
        functools.partial(expert_kernel, len(blocks)),
        out_shape=(half, half),
        in_specs=[VMEM_SPEC] * (len(blocks) + 3),
        out_specs=(VMEM_SPEC, VMEM_SPEC),
        scratch_shapes=[pltpu.VMEM((rows, width), jnp.bfloat16)],
        compiler_params=pltpu.CompilerParams(vmem_limit_bytes=24 * MIB),
        cost_estimate=pl.CostEstimate(
            flops=flops // 20, bytes_accessed=1024, transcendentals=0
        ),
        name="apply_experts",
    )(*blocks, *weights)


def wide(array):
    return array.astype(jnp.float32)


def local(token_codes, route_devices, route_members, gate_scores, gate_core, up_core, down_core):
    size = lax.axis_size("expert")
    local_experts = gate_core.shape[0]
    rows = token_codes.shape[0]
    weights = (gate_core, up_core, down_core)

    def exchange(array, mask):
        return lax.ppermute(array, "expert", [(i, i ^ mask) for i in range(size)])

    own = tag_tokens(
        token_codes, route_devices, route_members, gate_scores, local_experts, local_experts * size
    )
    def partial_sums(blocks):
        blocks = blocks + tuple(exchange(block, 1) for block in blocks)
        return apply_experts(blocks, weights)

    def paired(near, far):
        return wide(near) + wide(exchange(far, 1))

    def narrow(array):
        return array.astype(jnp.bfloat16)

    across, beside, beyond = exchange(own, 2), exchange(own, 4), exchange(own, 8)
    beside, beyond, own_too, across = lax.optimization_barrier((beside, beyond, own, across))
    middle = exchange(jnp.concatenate([beside, beyond]), 2)
    gathered = {3: exchange(beyond, 4)}
    for j in range(4, size // 4):
        low = j & -j
        gathered[j] = exchange(own if j == low else gathered[j - low], 4 * low)
    sums = {0: partial_sums((own_too, across))}
    middle, gathered[3], near = lax.optimization_barrier((middle, gathered[3], sums[0][0]))
    sums[0] = (near, sums[0][1])
    sums[1] = partial_sums((beside, middle[:rows]))
    sums[2] = partial_sums((beyond, middle[rows:]))
    for j, block in gathered.items():
        sums[j] = partial_sums((block, exchange(block, 2)))
    pair, other = paired(*sums[0]), paired(*sums[1])
    back = wide(exchange(narrow(jnp.concatenate([pair[rows:], other[rows:]])), 2))
    mixed = pair[:rows] + back[:rows] + wide(exchange(narrow(other[:rows] + back[rows:]), 4))
    for j in range(2, size // 4):
        pair = paired(*sums[j])
        done = pair[:rows] + wide(exchange(narrow(pair[rows:]), 2))
        mixed = mixed + wide(exchange(narrow(done), 4 * j))
    return mixed.astype(jnp.bfloat16)


def solution(mesh):
    tokens = P(("groups", "expert"), None)
    experts = P("expert", None, None)
    return jax.shard_map(
        local,
        mesh=mesh,
        in_specs=(tokens,) * 4 + (experts,) * 3,
        out_specs=tokens,
        check_vma=False,
    )
```

```python
import functools

import jax
import jax.numpy as jnp
from jax import lax
from jax.experimental import pallas as pl
from jax.experimental.pallas import tpu as pltpu
from jax.sharding import PartitionSpec as P

LANES = 128
MIB = 1024 * 1024
VMEM_SPEC = pl.BlockSpec(memory_space=pltpu.VMEM)


def tag_kernel(local_experts, codes_ref, devices_ref, members_ref, scores_ref, out_ref):
    rows, rank_in = codes_ref.shape
    lanes = out_ref.shape[1] - rank_in
    ids = devices_ref[...] * local_experts + members_ref[...]
    scores = scores_ref[...].astype(jnp.float32)
    expert = lax.broadcasted_iota(jnp.int32, (lanes, rows), 0)
    spread = jnp.zeros((lanes, rows), jnp.float32)
    for k in range(ids.shape[0]):
        spread = jnp.where(expert == ids[k : k + 1, :], scores[k : k + 1, :], spread)
    out_ref[:, :rank_in] = codes_ref[...]
    out_ref[:, rank_in:] = spread.T.astype(jnp.bfloat16)


def tag_tokens(codes, devices, members, scores, local_experts, experts):
    lanes = -(-experts // LANES) * LANES
    rows, rank_in = codes.shape
    operands = [
        pltpu.with_memory_space_constraint(operand, pltpu.HBM)
        for operand in (codes, devices.T, members.T, scores.T)
    ]
    return pl.pallas_call(
        functools.partial(tag_kernel, local_experts),
        out_shape=jax.ShapeDtypeStruct((rows, rank_in + lanes), jnp.bfloat16),
        out_specs=VMEM_SPEC,
        compiler_params=pltpu.CompilerParams(vmem_limit_bytes=8 * MIB),
        cost_estimate=pl.CostEstimate(
            flops=8_000_000_000, bytes_accessed=16_000_000, transcendentals=0
        ),
        name="tag_tokens",
    )(*operands)


def expert_kernel(count, *refs):
    blocks, (gate_ref, up_ref, down_ref, near_ref, far_ref, rows_ref) = refs[:count], refs[count:]
    local_experts, rank_in, hidden_units = gate_ref.shape
    at = 0
    for block in blocks:
        rows_ref[at : at + block.shape[0], :] = block[...]
        at += block.shape[0]
    scores = rows_ref[:, rank_in:].astype(jnp.float32)
    total = jnp.sum(scores, axis=1, keepdims=True)
    lane = lax.broadcasted_iota(jnp.int32, scores.shape, 1)
    first = lax.axis_index("expert") * local_experts
    codes = rows_ref[:, :rank_in]
    out = jnp.zeros((codes.shape[0], down_ref.shape[2]), jnp.float32)
    own = jnp.zeros_like(total)
    for e in range(local_experts):
        score = jnp.sum(jnp.where(lane == first + e, scores, 0.0), axis=1, keepdims=True)
        own = own + score
        gate = jnp.dot(codes, gate_ref[e], preferred_element_type=jnp.float32)
        up = jnp.dot(codes, up_ref[e], preferred_element_type=jnp.float32)
        hidden = gate / (1.0 + jnp.exp(-gate)) * up
        hidden = jnp.where(score > 0.0, hidden, 0.0).astype(jnp.bfloat16)
        out = out + jnp.dot(hidden, down_ref[e], preferred_element_type=jnp.float32)
    weight = 2.5 * own / total
    out = (weight * out.astype(jnp.bfloat16).astype(jnp.float32)).astype(jnp.bfloat16)
    half = near_ref.shape[0]
    near_ref[...] = out[:half]
    far_ref[...] = out[half:]


def apply_experts(blocks, weights):
    width = blocks[0].shape[1]
    rows = sum(block.shape[0] for block in blocks)
    local_experts, rank_in, hidden_units = weights[0].shape
    rank_out = weights[2].shape[2]
    half = jax.ShapeDtypeStruct((rows // 2, rank_out), jnp.bfloat16)
    flops = 2 * rows * local_experts * hidden_units * (2 * rank_in + rank_out)
    return pl.pallas_call(
        functools.partial(expert_kernel, len(blocks)),
        out_shape=(half, half),
        in_specs=[VMEM_SPEC] * (len(blocks) + 3),
        out_specs=(VMEM_SPEC, VMEM_SPEC),
        scratch_shapes=[pltpu.VMEM((rows, width), jnp.bfloat16)],
        compiler_params=pltpu.CompilerParams(vmem_limit_bytes=24 * MIB),
        cost_estimate=pl.CostEstimate(
            flops=flops // 20, bytes_accessed=1024, transcendentals=0
        ),
        name="apply_experts",
    )(*blocks, *weights)


def wide(array):
    return array.astype(jnp.float32)


def local(token_codes, route_devices, route_members, gate_scores, gate_core, up_core, down_core):
    size = lax.axis_size("expert")
    local_experts = gate_core.shape[0]
    rows = token_codes.shape[0]
    weights = (gate_core, up_core, down_core)

    def exchange(array, mask):
        return lax.ppermute(array, "expert", [(i, i ^ mask) for i in range(size)])

    own = tag_tokens(
        token_codes, route_devices, route_members, gate_scores, local_experts, local_experts * size
    )
    def partial_sums(blocks):
        blocks = blocks + tuple(exchange(block, 1) for block in blocks)
        return apply_experts(blocks, weights)

    def paired(near, far):
        return wide(near) + wide(exchange(far, 1))

    def narrow(array):
        return array.astype(jnp.bfloat16)

    def after(value, *arrays):
        return lax.optimization_barrier((*arrays, value))[:-1]

    across, beside, beyond = exchange(own, 2), exchange(own, 4), exchange(own, 8)
    near, far = partial_sums((own,))
    start = paired(near, far)
    gathered = {2: beyond, 3: exchange(beyond, 4)}
    for j in range(4, size // 4):
        low = j & -j
        gathered[j] = exchange(own if j == low else gathered[j - low], 4 * low)
    (corner,) = after(beyond, exchange(beside, 2))
    y2 = exchange(beyond, 2)
    near, far = partial_sums((across, beside, corner))
    pair = paired(near, far)
    y2, gathered[3] = after(near, y2, gathered[3])
    y = {j: exchange(block, 2) for j, block in gathered.items() if j > 2} | {2: y2}
    sums = {}
    for j, block in gathered.items():
        last = y[j]
        sums[j] = partial_sums((block, last))
    back = wide(exchange(narrow(jnp.concatenate([pair[:rows], pair[2 * rows :]])), 2))
    mixed = start + back[:rows]
    mixed = mixed + wide(exchange(narrow(pair[rows : 2 * rows] + back[rows:]), 4))
    for j in range(2, size // 4):
        pair = paired(*sums[j])
        done = pair[:rows] + wide(exchange(narrow(pair[rows:]), 2))
        mixed = mixed + wide(exchange(narrow(done), 4 * j))
    return mixed.astype(jnp.bfloat16)


def solution(mesh):
    tokens = P(("groups", "expert"), None)
    experts = P("expert", None, None)
    return jax.shard_map(
        local,
        mesh=mesh,
        in_specs=(tokens,) * 4 + (experts,) * 3,
        out_specs=tokens,
        check_vma=False,
    )
```

```python
import functools

import jax
import jax.numpy as jnp
from jax import lax
from jax.experimental import pallas as pl
from jax.experimental.pallas import tpu as pltpu
from jax.sharding import PartitionSpec as P

LANES = 128
MIB = 1024 * 1024
VMEM_SPEC = pl.BlockSpec(memory_space=pltpu.VMEM)


def tag_kernel(local_experts, codes_ref, devices_ref, members_ref, scores_ref, out_ref):
    rows, rank_in = codes_ref.shape
    lanes = out_ref.shape[1] - rank_in
    ids = devices_ref[...] * local_experts + members_ref[...]
    scores = scores_ref[...].astype(jnp.float32)
    expert = lax.broadcasted_iota(jnp.int32, (lanes, rows), 0)
    spread = jnp.zeros((lanes, rows), jnp.float32)
    for k in range(ids.shape[0]):
        spread = jnp.where(expert == ids[k : k + 1, :], scores[k : k + 1, :], spread)
    out_ref[:, :rank_in] = codes_ref[...]
    out_ref[:, rank_in:] = spread.T.astype(jnp.bfloat16)


def tag_tokens(codes, devices, members, scores, local_experts, experts):
    lanes = -(-experts // LANES) * LANES
    rows, rank_in = codes.shape
    operands = [
        pltpu.with_memory_space_constraint(operand, pltpu.HBM)
        for operand in (codes, devices.T, members.T, scores.T)
    ]
    return pl.pallas_call(
        functools.partial(tag_kernel, local_experts),
        out_shape=jax.ShapeDtypeStruct((rows, rank_in + lanes), jnp.bfloat16),
        out_specs=VMEM_SPEC,
        compiler_params=pltpu.CompilerParams(vmem_limit_bytes=8 * MIB),
        cost_estimate=pl.CostEstimate(
            flops=8_000_000_000, bytes_accessed=16_000_000, transcendentals=0
        ),
        name="tag_tokens",
    )(*operands)


def expert_kernel(count, *refs):
    blocks, (gate_ref, up_ref, down_ref, near_ref, far_ref, rows_ref) = refs[:count], refs[count:]
    local_experts, rank_in, hidden_units = gate_ref.shape
    at = 0
    for block in blocks:
        rows_ref[at : at + block.shape[0], :] = block[...]
        at += block.shape[0]
    scores = rows_ref[:, rank_in:].astype(jnp.float32)
    total = jnp.sum(scores, axis=1, keepdims=True)
    lane = lax.broadcasted_iota(jnp.int32, scores.shape, 1)
    first = lax.axis_index("expert") * local_experts
    codes = rows_ref[:, :rank_in]
    out = jnp.zeros((codes.shape[0], down_ref.shape[2]), jnp.float32)
    own = jnp.zeros_like(total)
    for e in range(local_experts):
        score = jnp.sum(jnp.where(lane == first + e, scores, 0.0), axis=1, keepdims=True)
        own = own + score
        gate = jnp.dot(codes, gate_ref[e], preferred_element_type=jnp.float32)
        up = jnp.dot(codes, up_ref[e], preferred_element_type=jnp.float32)
        hidden = gate / (1.0 + jnp.exp(-gate)) * up
        hidden = jnp.where(score > 0.0, hidden, 0.0).astype(jnp.bfloat16)
        out = out + jnp.dot(hidden, down_ref[e], preferred_element_type=jnp.float32)
    weight = 2.5 * own / total
    out = (weight * out.astype(jnp.bfloat16).astype(jnp.float32)).astype(jnp.bfloat16)
    half = near_ref.shape[0]
    near_ref[...] = out[:half]
    far_ref[...] = out[half:]


def apply_experts(blocks, weights):
    width = blocks[0].shape[1]
    rows = sum(block.shape[0] for block in blocks)
    local_experts, rank_in, hidden_units = weights[0].shape
    rank_out = weights[2].shape[2]
    half = jax.ShapeDtypeStruct((rows // 2, rank_out), jnp.bfloat16)
    flops = 2 * rows * local_experts * hidden_units * (2 * rank_in + rank_out)
    return pl.pallas_call(
        functools.partial(expert_kernel, len(blocks)),
        out_shape=(half, half),
        in_specs=[VMEM_SPEC] * (len(blocks) + 3),
        out_specs=(VMEM_SPEC, VMEM_SPEC),
        scratch_shapes=[pltpu.VMEM((rows, width), jnp.bfloat16)],
        compiler_params=pltpu.CompilerParams(vmem_limit_bytes=24 * MIB),
        cost_estimate=pl.CostEstimate(
            flops=flops // 20, bytes_accessed=1024, transcendentals=0
        ),
        name="apply_experts",
    )(*blocks, *weights)


def wide(array):
    return array.astype(jnp.float32)


def local(token_codes, route_devices, route_members, gate_scores, gate_core, up_core, down_core):
    size = lax.axis_size("expert")
    local_experts = gate_core.shape[0]
    rows = token_codes.shape[0]
    weights = (gate_core, up_core, down_core)

    def exchange(array, mask):
        return lax.ppermute(array, "expert", [(i, i ^ mask) for i in range(size)])

    own = tag_tokens(
        token_codes, route_devices, route_members, gate_scores, local_experts, local_experts * size
    )
    def partial_sums(blocks):
        blocks = blocks + tuple(exchange(block, 1) for block in blocks)
        return apply_experts(blocks, weights)

    def paired(near, far):
        return wide(near) + wide(exchange(far, 1))

    def narrow(array):
        return array.astype(jnp.bfloat16)

    def after(value, *arrays):
        return lax.optimization_barrier((*arrays, value))[:-1]

    across, beside, beyond = exchange(own, 2), exchange(own, 4), exchange(own, 8)
    near, far = partial_sums((own,))
    start = paired(near, far)
    (across,) = after(near, across)
    gathered = {2: beyond, 3: exchange(beyond, 4)}
    for j in range(4, size // 4):
        low = j & -j
        gathered[j] = exchange(own if j == low else gathered[j - low], 4 * low)
    (corner,) = after(beyond, exchange(beside, 2))
    y2 = exchange(beyond, 2)
    near, far = partial_sums((across, beside, corner))
    pair = paired(near, far)
    y2, gathered[3] = after(near, y2, gathered[3])
    y = {j: exchange(block, 2) for j, block in gathered.items() if j > 2} | {2: y2}
    sums = {}
    for j, block in gathered.items():
        last = y[j]
        sums[j] = partial_sums((block, last))
    back = wide(exchange(narrow(jnp.concatenate([pair[:rows], pair[2 * rows :]])), 2))
    mixed = start + back[:rows]
    mixed = mixed + wide(exchange(narrow(pair[rows : 2 * rows] + back[rows:]), 4))
    for j in range(2, size // 4):
        pair = paired(*sums[j])
        done = pair[:rows] + wide(exchange(narrow(pair[rows:]), 2))
        mixed = mixed + wide(exchange(narrow(done), 4 * j))
    return mixed.astype(jnp.bfloat16)


def solution(mesh):
    tokens = P(("groups", "expert"), None)
    experts = P("expert", None, None)
    return jax.shard_map(
        local,
        mesh=mesh,
        in_specs=(tokens,) * 4 + (experts,) * 3,
        out_specs=tokens,
        check_vma=False,
    )
```

```python
import functools

import jax
import jax.numpy as jnp
from jax import lax
from jax.experimental import pallas as pl
from jax.experimental.pallas import tpu as pltpu
from jax.sharding import PartitionSpec as P

LANES = 128
MIB = 1024 * 1024
VMEM_SPEC = pl.BlockSpec(memory_space=pltpu.VMEM)


def tag_kernel(local_experts, experts, codes_ref, devices_ref, members_ref, scores_ref, out_ref):
    rows, rank_in = codes_ref.shape
    fold = LANES // experts
    part = rows // fold
    ids = devices_ref[...] * local_experts + members_ref[...]
    scores = scores_ref[...].astype(jnp.float32)
    expert = lax.broadcasted_iota(jnp.int32, (experts, part), 0)
    pieces = []
    for q in range(fold):
        tokens = slice(q * part, (q + 1) * part)
        spread = jnp.zeros((experts, part), jnp.float32)
        for k in range(ids.shape[0]):
            spread = jnp.where(expert == ids[k : k + 1, tokens], scores[k : k + 1, tokens], spread)
        pieces.append(spread)
    for c in range(rank_in // LANES):
        out_ref[c * rows : (c + 1) * rows, :] = codes_ref[:, c * LANES : (c + 1) * LANES]
    packed = jnp.concatenate(pieces, axis=0).T
    out_ref[rank_in // LANES * rows :, :] = packed.astype(jnp.bfloat16)


def tag_tokens(codes, devices, members, scores, local_experts, experts):
    rows, rank_in = codes.shape
    operands = [
        pltpu.with_memory_space_constraint(operand, pltpu.HBM)
        for operand in (codes, devices.T, members.T, scores.T)
    ]
    height = rank_in // LANES * rows + rows * experts // LANES
    return pl.pallas_call(
        functools.partial(tag_kernel, local_experts, experts),
        out_shape=jax.ShapeDtypeStruct((height, LANES), jnp.bfloat16),
        out_specs=VMEM_SPEC,
        compiler_params=pltpu.CompilerParams(vmem_limit_bytes=8 * MIB),
        cost_estimate=pl.CostEstimate(
            flops=8_000_000_000, bytes_accessed=16_000_000, transcendentals=0
        ),
        name="tag_tokens",
    )(*operands)


def expert_kernel(count, experts, *refs):
    blocks, (gate_ref, up_ref, down_ref, near_ref, far_ref, rows_ref) = refs[:count], refs[count:]
    local_experts, rank_in, hidden_units = gate_ref.shape
    size = rows_ref.shape[0] // count
    fold = LANES // experts
    part = size // fold
    for i, block in enumerate(blocks):
        for c in range(rank_in // LANES):
            rows_ref[i * size : (i + 1) * size, c * LANES : (c + 1) * LANES] = block[
                c * size : (c + 1) * size, :
            ]
    packed = [block[rank_in // LANES * size :, :].astype(jnp.float32) for block in blocks]
    packed = jnp.concatenate(packed, axis=0)
    lane = lax.broadcasted_iota(jnp.int32, packed.shape, 1)
    first = lax.axis_index("expert") * local_experts

    def per_row(select):
        sums = [
            jnp.sum(jnp.where(select(q), packed, 0.0), axis=1, keepdims=True) for q in range(fold)
        ]
        return jnp.concatenate(
            [sums[q][i * part : (i + 1) * part] for i in range(count) for q in range(fold)], axis=0
        )

    total = per_row(lambda q: (lane >= q * experts) & (lane < (q + 1) * experts))
    codes = rows_ref[...]
    out = jnp.zeros((codes.shape[0], down_ref.shape[2]), jnp.float32)
    own = jnp.zeros_like(total)
    for e in range(local_experts):
        score = per_row(lambda q: lane == q * experts + first + e)
        own = own + score
        gate = jnp.dot(codes, gate_ref[e], preferred_element_type=jnp.float32)
        up = jnp.dot(codes, up_ref[e], preferred_element_type=jnp.float32)
        hidden = gate / (1.0 + jnp.exp(-gate)) * up
        hidden = jnp.where(score > 0.0, hidden, 0.0).astype(jnp.bfloat16)
        out = out + jnp.dot(hidden, down_ref[e], preferred_element_type=jnp.float32)
    weight = 2.5 * own / total
    out = (weight * out.astype(jnp.bfloat16).astype(jnp.float32)).astype(jnp.bfloat16)
    half = near_ref.shape[0]
    near_ref[...] = out[:half]
    far_ref[...] = out[half:]


def apply_experts(blocks, weights, size, experts):
    local_experts, rank_in, hidden_units = weights[0].shape
    rows = size * len(blocks)
    rank_out = weights[2].shape[2]
    half = jax.ShapeDtypeStruct((rows // 2, rank_out), jnp.bfloat16)
    flops = 2 * rows * local_experts * hidden_units * (2 * rank_in + rank_out)
    return pl.pallas_call(
        functools.partial(expert_kernel, len(blocks), experts),
        out_shape=(half, half),
        in_specs=[VMEM_SPEC] * (len(blocks) + 3),
        out_specs=(VMEM_SPEC, VMEM_SPEC),
        scratch_shapes=[pltpu.VMEM((rows, rank_in), jnp.bfloat16)],
        compiler_params=pltpu.CompilerParams(vmem_limit_bytes=24 * MIB),
        cost_estimate=pl.CostEstimate(
            flops=flops // 20, bytes_accessed=1024, transcendentals=0
        ),
        name="apply_experts",
    )(*blocks, *weights)


def wide(array):
    return array.astype(jnp.float32)


def local(token_codes, route_devices, route_members, gate_scores, gate_core, up_core, down_core):
    size = lax.axis_size("expert")
    local_experts = gate_core.shape[0]
    rows = token_codes.shape[0]
    weights = (gate_core, up_core, down_core)

    def exchange(array, mask):
        return lax.ppermute(array, "expert", [(i, i ^ mask) for i in range(size)])

    own = tag_tokens(
        token_codes, route_devices, route_members, gate_scores, local_experts, local_experts * size
    )
    def partial_sums(blocks):
        blocks = blocks + tuple(exchange(block, 1) for block in blocks)
        return apply_experts(blocks, weights, rows, local_experts * size)

    def paired(near, far):
        return wide(near) + wide(exchange(far, 1))

    def narrow(array):
        return array.astype(jnp.bfloat16)

    def after(value, *arrays):
        return lax.optimization_barrier((*arrays, value))[:-1]

    across, beside, beyond = exchange(own, 2), exchange(own, 4), exchange(own, 8)
    near, far = partial_sums((own,))
    start = paired(near, far)
    (across,) = after(near, across)
    gathered = {2: beyond, 3: exchange(beyond, 4)}
    for j in range(4, size // 4):
        low = j & -j
        gathered[j] = exchange(own if j == low else gathered[j - low], 4 * low)
    (corner,) = after(beyond, exchange(beside, 2))
    y2 = exchange(beyond, 2)
    near, far = partial_sums((across, beside, corner))
    pair = paired(near, far)
    y2, gathered[3] = after(near, y2, gathered[3])
    y = {j: exchange(block, 2) for j, block in gathered.items() if j > 2} | {2: y2}
    sums = {}
    for j, block in gathered.items():
        last = y[j]
        sums[j] = partial_sums((block, last))
    back = wide(exchange(narrow(jnp.concatenate([pair[:rows], pair[2 * rows :]])), 2))
    mixed = start + back[:rows]
    mixed = mixed + wide(exchange(narrow(pair[rows : 2 * rows] + back[rows:]), 4))
    for j in range(2, size // 4):
        pair = paired(*sums[j])
        done = pair[:rows] + wide(exchange(narrow(pair[rows:]), 2))
        mixed = mixed + wide(exchange(narrow(done), 4 * j))
    return mixed.astype(jnp.bfloat16)


def solution(mesh):
    tokens = P(("groups", "expert"), None)
    experts = P("expert", None, None)
    return jax.shard_map(
        local,
        mesh=mesh,
        in_specs=(tokens,) * 4 + (experts,) * 3,
        out_specs=tokens,
        check_vma=False,
    )
```

```python
import functools

import jax
import jax.numpy as jnp
from jax import lax
from jax.experimental import pallas as pl
from jax.experimental.pallas import tpu as pltpu
from jax.sharding import PartitionSpec as P

LANES = 128
MIB = 1024 * 1024
VMEM_SPEC = pl.BlockSpec(memory_space=pltpu.VMEM)


def tag_kernel(local_experts, experts, codes_ref, devices_ref, members_ref, scores_ref, out_ref):
    rows, rank_in = codes_ref.shape
    fold = LANES // experts
    part = rows // fold
    ids = devices_ref[...] * local_experts + members_ref[...]
    scores = scores_ref[...].astype(jnp.float32)
    expert = lax.broadcasted_iota(jnp.int32, (experts, part), 0)
    pieces = []
    for q in range(fold):
        tokens = slice(q * part, (q + 1) * part)
        spread = jnp.zeros((experts, part), jnp.float32)
        for k in range(ids.shape[0]):
            spread = jnp.where(expert == ids[k : k + 1, tokens], scores[k : k + 1, tokens], spread)
        pieces.append(spread)
    for c in range(rank_in // LANES):
        out_ref[c * rows : (c + 1) * rows, :] = codes_ref[:, c * LANES : (c + 1) * LANES]
    packed = jnp.concatenate(pieces, axis=0).T
    out_ref[rank_in // LANES * rows :, :] = packed.astype(jnp.bfloat16)


def tag_tokens(codes, devices, members, scores, local_experts, experts):
    rows, rank_in = codes.shape
    operands = [
        pltpu.with_memory_space_constraint(operand, pltpu.HBM)
        for operand in (codes, devices.T, members.T, scores.T)
    ]
    height = rank_in // LANES * rows + rows * experts // LANES
    return pl.pallas_call(
        functools.partial(tag_kernel, local_experts, experts),
        out_shape=jax.ShapeDtypeStruct((height, LANES), jnp.bfloat16),
        out_specs=VMEM_SPEC,
        compiler_params=pltpu.CompilerParams(vmem_limit_bytes=8 * MIB),
        cost_estimate=pl.CostEstimate(
            flops=8_000_000_000, bytes_accessed=16_000_000, transcendentals=0
        ),
        name="tag_tokens",
    )(*operands)


def expert_kernel(count, experts, *refs):
    blocks, (gate_ref, up_ref, down_ref, near_ref, far_ref, rows_ref) = refs[:count], refs[count:]
    local_experts, rank_in, hidden_units = gate_ref.shape
    size = rows_ref.shape[0] // count
    fold = LANES // experts
    part = size // fold
    for i, block in enumerate(blocks):
        for c in range(rank_in // LANES):
            rows_ref[i * size : (i + 1) * size, c * LANES : (c + 1) * LANES] = block[
                c * size : (c + 1) * size, :
            ]
    packed = jnp.concatenate([block[rank_in // LANES * size :, :] for block in blocks], axis=0)
    first = lax.axis_index("expert") * local_experts
    lane = lax.broadcasted_iota(jnp.int32, (LANES, LANES), 0)
    column = lax.broadcasted_iota(jnp.int32, (LANES, LANES), 1)
    shift = fold.bit_length() - 1
    inside, kind = lane - (column & (fold - 1)) * experts, column >> shift
    whole = (kind == 0) & (inside >= 0) & (inside < experts)
    taken = whole | ((kind > 0) & (inside == first + kind - 1))
    picked = jnp.dot(
        packed, jnp.where(taken, 1.0, 0.0).astype(jnp.bfloat16), preferred_element_type=jnp.float32
    )

    def per_row(kind):
        return jnp.concatenate(
            [
                picked[i * part : (i + 1) * part, kind * fold + q : kind * fold + q + 1]
                for i in range(count)
                for q in range(fold)
            ],
            axis=0,
        )

    total = per_row(0)
    codes = rows_ref[...]
    out = jnp.zeros((codes.shape[0], down_ref.shape[2]), jnp.float32)
    own = jnp.zeros_like(total)
    for e in range(local_experts):
        score = per_row(1 + e)
        own = own + score
        gate = jnp.dot(codes, gate_ref[e], preferred_element_type=jnp.float32)
        up = jnp.dot(codes, up_ref[e], preferred_element_type=jnp.float32)
        hidden = gate / (1.0 + jnp.exp(-gate)) * up
        hidden = jnp.where(score > 0.0, hidden, 0.0).astype(jnp.bfloat16)
        out = out + jnp.dot(hidden, down_ref[e], preferred_element_type=jnp.float32)
    weight = 2.5 * own / total
    out = (weight * out.astype(jnp.bfloat16).astype(jnp.float32)).astype(jnp.bfloat16)
    half = near_ref.shape[0]
    near_ref[...] = out[:half]
    far_ref[...] = out[half:]


def apply_experts(blocks, weights, size, experts):
    local_experts, rank_in, hidden_units = weights[0].shape
    rows = size * len(blocks)
    rank_out = weights[2].shape[2]
    half = jax.ShapeDtypeStruct((rows // 2, rank_out), jnp.bfloat16)
    flops = 2 * rows * local_experts * hidden_units * (2 * rank_in + rank_out)
    return pl.pallas_call(
        functools.partial(expert_kernel, len(blocks), experts),
        out_shape=(half, half),
        in_specs=[VMEM_SPEC] * (len(blocks) + 3),
        out_specs=(VMEM_SPEC, VMEM_SPEC),
        scratch_shapes=[pltpu.VMEM((rows, rank_in), jnp.bfloat16)],
        compiler_params=pltpu.CompilerParams(vmem_limit_bytes=24 * MIB),
        cost_estimate=pl.CostEstimate(
            flops=flops // 20, bytes_accessed=1024, transcendentals=0
        ),
        name="apply_experts",
    )(*blocks, *weights)


def wide(array):
    return array.astype(jnp.float32)


def local(token_codes, route_devices, route_members, gate_scores, gate_core, up_core, down_core):
    size = lax.axis_size("expert")
    local_experts = gate_core.shape[0]
    rows = token_codes.shape[0]
    weights = (gate_core, up_core, down_core)

    def exchange(array, mask):
        return lax.ppermute(array, "expert", [(i, i ^ mask) for i in range(size)])

    own = tag_tokens(
        token_codes, route_devices, route_members, gate_scores, local_experts, local_experts * size
    )
    def partial_sums(blocks):
        blocks = blocks + tuple(exchange(block, 1) for block in blocks)
        return apply_experts(blocks, weights, rows, local_experts * size)

    def paired(near, far):
        return wide(near) + wide(exchange(far, 1))

    def narrow(array):
        return array.astype(jnp.bfloat16)

    def after(value, *arrays):
        return lax.optimization_barrier((*arrays, value))[:-1]

    across, beside, beyond = exchange(own, 2), exchange(own, 4), exchange(own, 8)
    near, far = partial_sums((own,))
    start = paired(near, far)
    (across,) = after(near, across)
    gathered = {2: beyond, 3: exchange(beyond, 4)}
    for j in range(4, size // 4):
        low = j & -j
        gathered[j] = exchange(own if j == low else gathered[j - low], 4 * low)
    (corner,) = after(beyond, exchange(beside, 2))
    y2 = exchange(beyond, 2)
    near, far = partial_sums((across, beside, corner))
    pair = paired(near, far)
    y2, gathered[3] = after(near, y2, gathered[3])
    y = {j: exchange(block, 2) for j, block in gathered.items() if j > 2} | {2: y2}
    sums = {}
    for j, block in gathered.items():
        last = y[j]
        sums[j] = partial_sums((block, last))
    back = wide(exchange(narrow(jnp.concatenate([pair[:rows], pair[2 * rows :]])), 2))
    mixed = start + back[:rows]
    mixed = mixed + wide(exchange(narrow(pair[rows : 2 * rows] + back[rows:]), 4))
    for j in range(2, size // 4):
        pair = paired(*sums[j])
        done = pair[:rows] + wide(exchange(narrow(pair[rows:]), 2))
        mixed = mixed + wide(exchange(narrow(done), 4 * j))
    return mixed.astype(jnp.bfloat16)


def solution(mesh):
    tokens = P(("groups", "expert"), None)
    experts = P("expert", None, None)
    return jax.shard_map(
        local,
        mesh=mesh,
        in_specs=(tokens,) * 4 + (experts,) * 3,
        out_specs=tokens,
        check_vma=False,
    )
```
